512 devices in a mesh: dp: 32 (over z, y_lo), module: 16 (over x, y_hi, core).
Axes of the slice: x: 4, y: 4 (y_hi: 2, y_lo: 2; y = y_hi * 2 + y_lo), z: 16, core: 2. Of those that a mesh axis runs over, the one named last changes fastest.
Arguments:
- act_factors: bfloat16 [8192, 16, 32, 128], P(('dp', 'module')), may hold values from -6 to 6
- grad_factors: bfloat16 [8192, 16, 32, 128], P(('dp', 'module')), may hold values from -6 to 6
- lengths: int32 [8192], P(('dp', 'module')), may hold values from 1 to 128, 786432 in all
- module_slot: int32 [16], replicated, may hold values from 0 to 15, each once
- query_grads: float32 [16, 1024, 512], P('module', 'dp'), may hold values from -4 to 4
Outputs:
- scores: float32 [8192, 512], P('dp', 'module')
The draws below stay inside these ranges and needn't reach their ends.
Inputs may be any that keep to these rules, and one draw needn't show every extreme that they name: `module_slot`: each module is held by exactly one index of the module axis. `lengths`: some example has all 128 tokens.
All inputs are finite; a program needn't handle non-finite values. No bound on the sum of `lengths` on one device may be relied on, other than what follows from the above.
Results may differ from the reference program's by a relative error of at most 0.007.
Values may be sent and summed in bfloat16 or wider, within the bound.
A program may use at most 64 MiB of HBM per device.

```python
import math
import jax
import jax.numpy as jnp
import numpy as np
from jax import lax

RANK = 32
PROJ = 1024
LEN = 128
QUERIES = 512
ITERS = 4
MODS = 16
EXAMPLES = 8192


def block_scale(own_key, extent, pieces, low, high):
    def one(dim, parts):
        heights = jax.random.uniform(jax.random.fold_in(jax.random.fold_in(own_key, 6), dim), (parts,), jnp.float32, low / len(pieces), high / len(pieces))
        return jnp.repeat(jnp.exp(heights), extent[dim] // parts).reshape((-1,) + (1,) * (len(extent) - dim - 1))

    loudness = one(*pieces[0])
    for cut in pieces[1:]:
        loudness = loudness * one(*cut)
    return loudness


def length_profile(count, total, most, skew):
    portions = [(1 << 20) // math.isqrt(rank ** skew) + 1 for rank in range(2, count + 1)]
    rest, holding = total - most - (count - 1), [1] * (count - 1)
    while rest > 0:
        free = [i for i in range(count - 1) if holding[i] < most]
        mass, budget = sum([portions[i] for i in free]), rest
        for i in free:
            extra = min(most - holding[i], max(1, budget * portions[i] // mass), rest)
            holding[i] = holding[i] + extra
            rest = rest - extra
    return np.array([most] + holding)


def ragged_sizes(own_key, number_of, total, most, lean):
    if number_of == 2:
        one = jax.random.randint(own_key, (), max(1, total - most), min(most, total - 1) + 1)
        return jnp.stack([one, total - one])
    sizes = jnp.asarray(length_profile(number_of, total, most, lean), jnp.int32)
    pairs = (number_of - 1) // 2
    source_of, taker = sizes[1:1 + 2 * pairs:2], sizes[2:2 + 2 * pairs:2]
    margin = jnp.minimum(source_of - 1, most - taker)
    moved = jax.random.randint(jax.random.fold_in(own_key, 1), (pairs,), 0, 1 << 20) % (margin + 1)
    sizes = sizes.at[1:1 + 2 * pairs:2].set(source_of - moved).at[2:2 + 2 * pairs:2].set(taker + moved)
    return sizes[jax.random.permutation(jax.random.fold_in(own_key, 2), number_of)]


def bell_draw(rng, extent, width, bound, cuts=(), kind=jnp.bfloat16):
    values = jax.random.normal(rng, extent, jnp.float32) * width
    if len(cuts) > 0:
        values = block_scale(rng, extent, cuts, -0.22, 0.18) * values
    return jnp.clip(values, min=-bound, max=bound).astype(kind)


def setup_inputs(seed: int = 0) -> dict:
    seeds = jax.random.split(jax.random.key(seed), 6)
    return {
        "act_factors": bell_draw(seeds[0], (EXAMPLES, MODS, RANK, LEN), 1.0, 6.0, ((0, 512),)),
        "grad_factors": bell_draw(seeds[1], (EXAMPLES, MODS, RANK, LEN), 1.0, 6.0, ((0, 512),)),
        "lengths": ragged_sizes(seeds[2], EXAMPLES, EXAMPLES * LEN * 3 // 4, LEN, 0).astype(jnp.int32),
        "module_slot": jax.random.permutation(seeds[3], MODS).astype(jnp.int32),
        "query_grads": bell_draw(seeds[4], (MODS, PROJ, QUERIES), 0.25, 4.0, ((0, 16), (1, 32)), jnp.float32),
    }


def chebyshev(rhs, multiply, damping, upper):
    center = (upper + damping) / 2.0
    radius = (upper - damping) / 2.0
    sigma = center / radius
    rho = 1.0 / sigma
    resid = rhs
    step = rhs / center
    solved = jnp.zeros_like(rhs)
    for index in range(ITERS):
        solved = solved + step
        if index + 1 < ITERS:
            resid = resid - (multiply(step) + damping * step)
            rho_next = 1.0 / (2.0 * sigma - rho)
            step = rho_next * rho * step + (2.0 * rho_next / radius) * resid
            rho = rho_next
    return solved


def reference(act_factors, grad_factors, lengths, module_slot, query_grads):
    holder = jnp.zeros((MODS,), jnp.int32).at[module_slot].set(jnp.arange(MODS, dtype=jnp.int32))
    live = (jnp.arange(LEN, dtype=jnp.int32)[None, :] < lengths[:, None]).astype(jnp.bfloat16)

    def per_slot(module):
        act = jnp.take(act_factors, module, axis=1) * live[:, None, :]
        grad = jnp.take(grad_factors, module, axis=1)
        outer = jnp.einsum("eil,ejl->eij", act.astype(jnp.float32), grad.astype(jnp.float32))
        train = outer.reshape(EXAMPLES, PROJ).astype(jnp.bfloat16)
        gram = jnp.dot(train.T, train, preferred_element_type=jnp.float32) / EXAMPLES
        return train, gram

    trains, grams = lax.map(per_slot, holder)
    traces = jnp.trace(grams, axis1=1, axis2=2)
    mean_eig = traces / PROJ
    damping = 0.1 * jnp.mean(mean_eig)

    def solve_slot(inputs):
        gram, queries, level = inputs

        def multiply(step):
            return jnp.dot(gram, step, precision=lax.Precision.HIGHEST, preferred_element_type=jnp.float32)

        return chebyshev(queries, multiply, damping, damping + 4.0 * level).astype(jnp.bfloat16)

    solved = lax.map(solve_slot, (grams, query_grads, mean_eig))

    def accumulate(total, pair):
        train, answer = pair
        return total + jnp.dot(train, answer, preferred_element_type=jnp.float32), None

    scores, unused = lax.scan(accumulate, jnp.zeros((EXAMPLES, QUERIES), jnp.float32), (trains, solved))
    return scores
```

```python
import functools

import jax
import jax.numpy as jnp
from jax import lax
from jax.experimental import pallas as pl
from jax.experimental.pallas import tpu as pltpu
from jax.sharding import PartitionSpec as P

ITERS = 4
MESH = pl.DeviceIdType.MESH
BF16 = jnp.bfloat16
F32 = jnp.float32


def kernel(
    planes,
    slot_ref,
    len_ref,
    act_hbm,
    grad_hbm,
    query_ref,
    out_ref,
    act,
    grad,
    prod,
    tsend,
    tall,
    gpart,
    gfull,
    up_out,
    up_in,
    down_out,
    down_in,
    qsrc,
    qfull,
    step_ref,
    resid_ref,
    acc_ref,
    ssend,
    srecv,
    slot_traces,
    plane_traces,
    diag_ref,
    load_sem,
    t_send,
    t_recv,
    tsib_send,
    tsib_recv,
    q_pair,
    q_send,
    q_recv,
    rs_send,
    rs_recv,
    g_send,
    g_recv,
    tr_send,
    tr_recv,
    trz_send,
    trz_recv,
    s_send,
    s_recv,
):
    per_dev, slots, rank, span = act.shape
    proj = rank * rank
    band = proj // (2 * planes)
    half_band = proj // 2
    rows = slots * per_dev
    queries = qfull.shape[1]
    per_owner = queries // slots
    up_steps = planes // 2
    down_steps = planes - 1 - up_steps
    examples = rows * 2 * planes

    dp, mod = lax.axis_index("dp"), lax.axis_index("module")
    z, y_lo = dp // 2, dp % 2
    core = mod % 2
    slot = (mod // 2) * 2 + y_lo
    above, below = (z + 1) % planes, (z + planes - 1) % planes

    def device(plane, chip, cc):
        return (plane * 2 + chip % 2, (chip // 2) * 2 + cc)

    def remote(src, dst, send, recv, target):
        return pltpu.make_async_remote_copy(
            src_ref=src, dst_ref=dst, send_sem=send, recv_sem=recv,
            device_id=target, device_id_type=MESH,
        )

    sibling = device(z, slot, 1 - core)
    up_dev, down_dev = device(above, slot, core), device(below, slot, core)

    loads = [
        pltpu.make_async_copy(act_hbm, act, load_sem.at[0]),
        pltpu.make_async_copy(grad_hbm, grad, load_sem.at[1]),
    ]
    for load in loads:
        load.start()

    barrier = pltpu.get_barrier_semaphore()

    def greet(index, carry):
        chip, cc = index // 2, index % 2

        @pl.when(jnp.logical_or(chip != slot, cc != core))
        def _():
            pl.semaphore_signal(
                barrier, inc=1, device_id=device(z, chip, cc), device_id_type=MESH
            )

        return carry

    lax.fori_loop(0, 2 * slots, greet, 0)
    for target in (up_dev, down_dev):
        pl.semaphore_signal(barrier, inc=1, device_id=target, device_id_type=MESH)
    qsrc[...] = query_ref[...].astype(BF16)
    pl.semaphore_wait(barrier, 2 * slots + 1)

    def q_rows(plane, cc):
        return qfull.at[pl.ds(pl.multiple_of((plane * 2 + cc) * band, band), band), :]

    paired = remote(
        qsrc,
        qfull.at[pl.ds(pl.multiple_of(dp * band, band), band), :],
        q_pair.at[0],
        q_pair.at[1],
        device(z, (slot // 2) * 2 + core, y_lo),
    )

    @pl.when(y_lo != core)
    def _():
        paired.start()

    @pl.when(y_lo == core)
    def _():
        qfull[pl.ds(pl.multiple_of(dp * band, band), band), :] = qsrc[...]

    def chain(part, send, recv, share):
        def up(t):
            block = part((z + planes - t) % planes, core)
            return remote(block, block, send.at[t], recv.at[t], up_dev)

        def down(t):
            block = part((z + t) % planes, core)
            return remote(
                block, block, send.at[up_steps + t], recv.at[up_steps + t], down_dev
            )

        def up_arrival(t):
            block = part((z + planes - t - 1) % planes, core)
            return remote(block, block, send.at[t], recv.at[t], up_dev)

        def down_arrival(t):
            block = part((z + t + 1) % planes, core)
            return remote(
                block, block, send.at[up_steps + t], recv.at[up_steps + t], down_dev
            )

        base = up_steps + down_steps

        def across(t):
            block = part((z + t) % planes, core)
            return remote(block, block, send.at[base + t], recv.at[base + t], sibling)

        def across_arrival(t):
            block = part((z + t) % planes, 1 - core)
            return remote(block, block, send.at[base + t], recv.at[base + t], sibling)

        def run(t):
            if t > 0:
                up_arrival(t - 1).wait_recv()
            if t < up_steps:
                up(t).start()
            if t > 0 and t - 1 < down_steps:
                down_arrival(t - 1).wait_recv()
            if t < down_steps:
                down(t).start()
            if share:
                if t == 0:
                    across(0).start()
                else:
                    across(planes - t).start()
                    if t - 1 < down_steps:
                        across(t).start()

        def finish():
            for t in range(up_steps):
                up(t).wait_send()
            for t in range(down_steps):
                down(t).wait_send()
            if share:
                for t in range(planes):
                    across_arrival(t).wait_recv()
                    across(t).wait_send()

        return run, finish

    q_run, q_finish = chain(q_rows, q_send, q_recv, True)

    for load in loads:
        load.wait()

    lanes = lax.broadcasted_iota(jnp.int32, (8, 4 * rank), 1) // rank
    positions = lax.broadcasted_iota(jnp.int32, (4 * rank, span), 1)

    def t_rows(chip, cc):
        first = cc * rows + (chip % 2) * (rows // 2) + (chip // 2) * per_dev
        return tall.at[pl.ds(pl.multiple_of(first, per_dev), per_dev), :]

    def holder(chip):
        found = jnp.int32(0)
        for index in range(slots):
            found = jnp.where(slot_ref[index] == chip, index, found)
        return found

    def group(k, carry):
        first = ((slot // 4 + 1 + k) % (slots // 4)) * 4
        held = [holder(first + r) for r in range(4)]
        for e in range(per_dev):
            left = jnp.concatenate([act[e, h] for h in held], axis=0)
            right = jnp.concatenate([grad[e, h] for h in held], axis=0)
            left = jnp.where(positions < len_ref[e], left, jnp.zeros_like(left))
            prod[pl.ds(e * 4 * rank, 4 * rank), :] = lax.dot_general(
                left, right, (((1,), (1,)), ((), ())), preferred_element_type=F32
            )
        for r in range(4):
            chip = first + r
            for g in range(proj // (4 * rank)):
                halves = []
                for h in range(per_dev // 8):
                    merged = None
                    for b in range(4):
                        row = h * 8 * 4 * rank + r * rank + 4 * g + b
                        piece = prod[pl.ds(row, 8, stride=4 * rank), :]
                        if b != r:
                            piece = pltpu.roll(piece, ((b - r) % 4) * rank, 1)
                        merged = piece if merged is None else jnp.where(lanes == b, piece, merged)
                    halves.append(merged)
                tsend[chip, :, pl.ds(g * 4 * rank, 4 * rank)] = jnp.concatenate(
                    halves, axis=0
                ).astype(BF16)

            @pl.when(chip != slot)
            def _():
                remote(
                    tsend.at[chip], t_rows(slot, core), t_send.at[chip], t_recv.at[slot],
                    device(z, chip, core),
                ).start()

            @pl.when(chip == slot)
            def _():
                first_row = core * rows + (slot % 2) * (rows // 2) + (slot // 2) * per_dev
                tall[pl.ds(pl.multiple_of(first_row, per_dev), per_dev), :] = tsend[chip]

        return carry

    lax.fori_loop(0, slots // 4, group, 0)

    @pl.when(y_lo != core)
    def _():
        paired.wait()

    def collect(k, carry):
        chip = (slot + k) % slots

        @pl.when(k > 0)
        def _():
            remote(
                t_rows(chip, core), t_rows(chip, core), t_send.at[chip], t_recv.at[chip], sibling
            ).wait_recv()

        remote(
            t_rows(chip, core), t_rows(chip, core), tsib_send.at[chip], tsib_recv.at[chip], sibling
        ).start()
        return carry

    for t in range(up_steps + 1):
        q_run(t)
    lax.fori_loop(0, slots, collect, 0)

    def collected(chip, carry):
        other = remote(
            t_rows(chip, 1 - core), t_rows(chip, 1 - core), tsib_send.at[chip], tsib_recv.at[chip],
            sibling,
        )
        other.wait_recv()
        other.wait_send()
        return carry

    lax.fori_loop(0, slots, collected, 0)

    mine = pl.ds(pl.multiple_of(core * half_band, half_band), half_band)
    gpart[...] = lax.dot_general(
        tall[:, mine], tall[...], (((0,), (0,)), ((), ())), preferred_element_type=F32
    )
    lane = min(128, half_band)
    off = lax.broadcasted_iota(jnp.int32, (lane, lane), 0) != lax.broadcasted_iota(
        jnp.int32, (lane, lane), 1
    )
    for n in range(half_band // lane):
        cols = pl.ds(pl.multiple_of(core * half_band + n * lane, lane), lane)
        gpart[pl.ds(n * lane, lane), cols] = jnp.where(off, gpart[pl.ds(n * lane, lane), cols], 0.0)

    def owned(plane):
        return gpart[pl.ds(pl.multiple_of(plane * band, band), band), :]

    def rs_up(t):
        return remote(up_out.at[t], up_in.at[t], rs_send.at[t], rs_recv.at[t], up_dev)

    def rs_down(t):
        return remote(
            down_out.at[t], down_in.at[t], rs_send.at[up_steps + t], rs_recv.at[up_steps + t],
            down_dev,
        )

    def trace_to(chip):
        return remote(
            slot_traces.at[slot], slot_traces.at[slot], tr_send.at[chip], tr_recv.at[slot],
            device(z, chip, core),
        )

    def trace_from(chip):
        return remote(
            slot_traces.at[chip], slot_traces.at[chip], tr_send.at[chip], tr_recv.at[chip], sibling
        )

    for t in range(up_steps):
        value = owned((z + up_steps - t) % planes)
        if t > 0:
            rs_up(t - 1).wait_recv()
            value = value + up_in[t - 1].astype(F32)
        up_out[t] = value.astype(BF16)
        rs_up(t).start()
        if t < down_steps:
            value = owned((z + planes - down_steps + t) % planes)
            if t > 0:
                rs_down(t - 1).wait_recv()
                value = value + down_in[t - 1].astype(F32)
            down_out[t] = value.astype(BF16)
            rs_down(t).start()
        if t == 0:
            squares = tall[...].astype(F32)
            squares = jnp.sum(squares * squares, axis=0, keepdims=True)
            for n in range(proj // 128):
                plane_traces[z, pl.ds(n, 1), :] = squares[:, n * 128 : (n + 1) * 128]
            squares = jnp.sum(squares, axis=1, keepdims=True)
            slot_traces[slot] = jnp.broadcast_to(squares, (8, 128))

            def tell(chip, carry):
                @pl.when(chip != slot)
                def _():
                    trace_to(chip).start()

                return carry

            lax.fori_loop(0, slots, tell, 0)

    def heard(chip, carry):
        @pl.when(chip != slot)
        def _():
            trace_from(chip).wait_recv()
            trace_to(chip).wait_send()

        return carry

    lax.fori_loop(0, slots, heard, 0)
    total = jnp.sum(slot_traces[...], axis=0)
    plane_traces[z, pl.ds(proj // 128, 8), :] = total

    def g_rows(plane, cc):
        return gfull.at[pl.ds(pl.multiple_of((cc * planes + plane) * band, band), band), :]

    value = owned(z)
    rs_up(up_steps - 1).wait_recv()
    value = value + up_in[up_steps - 1].astype(F32)
    if down_steps > 0:
        rs_down(down_steps - 1).wait_recv()
        value = value + down_in[down_steps - 1].astype(F32)
    gfull[pl.ds(pl.multiple_of((core * planes + z) * band, band), band), :] = value.astype(BF16)

    g_run, g_finish = chain(g_rows, g_send, g_recv, True)
    trz_run, trz_finish = chain(lambda plane, cc: plane_traces.at[plane], trz_send, trz_recv, False)
    for t in range(up_steps + 1):
        g_run(t)
        trz_run(t)
    for t in range(up_steps):
        rs_up(t).wait_send()
    for t in range(down_steps):
        rs_down(t).wait_send()

    def sent(chip, carry):
        @pl.when(chip != slot)
        def _():
            remote(
                tsend.at[chip], t_rows(slot, core), t_send.at[chip], t_recv.at[slot],
                device(z, chip, core),
            ).wait_send()

        return carry

    lax.fori_loop(0, slots, sent, 0)
    q_finish()
    trz_finish()
    g_finish()

    traces = jnp.sum(plane_traces[...], axis=0)
    diagonal = traces[: proj // 128] / examples
    own_eig = jnp.sum(jnp.sum(diagonal, axis=1, keepdims=True), axis=0, keepdims=True) / proj
    damping = 0.1 * (traces[proj // 128 : proj // 128 + 1, 0:1] / (examples * proj * slots))
    diag_ref[...] = jnp.concatenate([diagonal[n : n + 1] for n in range(proj // 128)], axis=1)
    upper = damping + 4.0 * own_eig
    center = (upper + damping) / 2.0
    radius = (upper - damping) / 2.0
    sigma = center / radius
    rho = 1.0 / sigma
    train = tall[pl.ds(pl.multiple_of(core * rows, rows), rows), :].astype(F32)
    resid_ref[...] = train
    step_ref[...] = train / center
    acc_ref[...] = step_ref[...]
    tile = min(256, proj)
    for index in range(ITERS - 1):
        rho_next = 1.0 / (2.0 * sigma - rho)
        rounded = step_ref[...].astype(BF16)

        def column(n, carry):
            cols = pl.ds(pl.multiple_of(n * tile, tile), tile)
            product = jnp.dot(rounded, gfull[:, cols], preferred_element_type=F32)
            step = step_ref[:, cols]
            resid = resid_ref[:, cols] - (product * (1.0 / examples) + (diag_ref[:, cols] + damping) * step)
            resid_ref[:, cols] = resid
            step = rho_next * rho * step + (2.0 * rho_next / radius) * resid
            step_ref[:, cols] = step
            acc_ref[:, cols] = acc_ref[:, cols] + step
            return carry

        lax.fori_loop(0, proj // tile, column, 0)
        rho = rho_next

    scores = jnp.dot(acc_ref[...].astype(BF16), qfull[...], preferred_element_type=F32)
    ssend[...] = scores.T.astype(BF16)

    def block(index):
        owner, low = index // 2, index % 2
        return ssend.at[
            pl.ds(pl.multiple_of(owner * per_owner, per_owner), per_owner),
            pl.ds(pl.multiple_of(low * (rows // 2), rows // 2), rows // 2),
        ]

    mark = slot * 2 + core

    def score_to(index):
        return remote(
            block(index), srecv.at[mark], s_send.at[index], s_recv.at[mark],
            (z * 2 + index % 2, index // 2),
        )

    own = mod * 2 + y_lo

    def push(k, carry):
        index = (own + k) % (2 * slots)
        score_to(index).start()
        return carry

    lax.fori_loop(1, 2 * slots, push, 0)
    srecv[mark] = ssend[
        pl.ds(pl.multiple_of(mod * per_owner, per_owner), per_owner),
        pl.ds(pl.multiple_of(y_lo * (rows // 2), rows // 2), rows // 2),
    ]

    def pull(k, carry):
        index = (mark + k) % (2 * slots)
        remote(
            srecv.at[index], srecv.at[index], s_send.at[index], s_recv.at[index], sibling
        ).wait_recv()
        return carry

    lax.fori_loop(1, 2 * slots, pull, 0)
    sums = []
    for cc in range(2):
        summed = srecv[cc].astype(F32)
        for chip in range(1, slots):
            summed = summed + srecv[chip * 2 + cc].astype(F32)
        sums.append(summed)
    width = rows // 2
    runs = width // per_dev
    lane_run = lax.broadcasted_iota(jnp.int32, (per_owner, width), 1) // per_dev
    for h in range(2):
        merged = jnp.zeros((per_owner, width), F32)
        for n in range(runs // 2):
            for cc in range(2):
                shift = (2 * n + cc - (h * (runs // 2) + n)) % runs
                piece = pltpu.roll(sums[cc], shift * per_dev, 1) if shift else sums[cc]
                merged = jnp.where(lane_run == 2 * n + cc, piece, merged)
        out_ref[:, pl.ds(h * width, width)] = merged

    def pushed(k, carry):
        score_to((own + k) % (2 * slots)).wait_send()
        return carry

    lax.fori_loop(1, 2 * slots, pushed, 0)


def per_device(planes, act_factors, grad_factors, lengths, module_slot, query_grads):
    per_dev, slots, rank, span = act_factors.shape
    proj = rank * rank
    rows = slots * per_dev
    band, queries = query_grads.shape[1:]
    per_owner = queries // slots
    up_steps = planes // 2
    down_steps = planes - 1 - up_steps
    sem = pltpu.SemaphoreType.DMA
    wide = planes - 1 + planes
    vmem = pltpu.VMEM
    result = pl.pallas_call(
        functools.partial(kernel, planes),
        out_shape=jax.ShapeDtypeStruct((per_owner, rows), F32),
        in_specs=[
            pl.BlockSpec(memory_space=pltpu.SMEM),
            pl.BlockSpec(memory_space=pltpu.SMEM),
            pl.BlockSpec(memory_space=pltpu.HBM),
            pl.BlockSpec(memory_space=pltpu.HBM),
            pl.BlockSpec(memory_space=pltpu.VMEM),
        ],
        out_specs=pl.BlockSpec(memory_space=pltpu.VMEM),
        scratch_shapes=[
            vmem((per_dev, slots, rank, span), BF16),
            vmem((per_dev, slots, rank, span), BF16),
            vmem((per_dev * 4 * rank, 4 * rank), F32),
            vmem((slots, per_dev, proj), BF16),
            vmem((2 * rows, proj), BF16),
            vmem((proj // 2, proj), F32),
            vmem((proj, proj), BF16),
            vmem((up_steps, band, proj), BF16),
            vmem((up_steps, band, proj), BF16),
            vmem((max(down_steps, 1), band, proj), BF16),
            vmem((max(down_steps, 1), band, proj), BF16),
            vmem((band, queries), BF16),
            vmem((proj, queries), BF16),
            vmem((rows, proj), F32),
            vmem((rows, proj), F32),
            vmem((rows, proj), F32),
            vmem((queries, rows), BF16),
            vmem((2 * slots, per_owner, rows // 2), BF16),
            vmem((slots, 8, 128), F32),
            vmem((planes, proj // 128 + 8, 128), F32),
            vmem((1, proj), F32),
            sem((2,)),
            sem((slots,)),
            sem((slots,)),
            sem((slots,)),
            sem((slots,)),
            sem((2,)),
            sem((wide,)),
            sem((wide,)),
            sem((planes - 1,)),
            sem((planes - 1,)),
            sem((wide,)),
            sem((wide,)),
            sem((slots,)),
            sem((slots,)),
            sem((planes - 1,)),
            sem((planes - 1,)),
            sem((2 * slots,)),
            sem((2 * slots,)),
        ],
        compiler_params=pltpu.CompilerParams(
            collective_id=0, has_side_effects=True, vmem_limit_bytes=62 * 1024 * 1024
        ),
    )(module_slot, lengths, act_factors, grad_factors, query_grads[0])
    return result.T


def solution(mesh):
    planes = mesh.shape["dp"] // 2
    return jax.shard_map(
        functools.partial(per_device, planes),
        mesh=mesh,
        in_specs=(
            P(("dp", "module"), None, None, None),
            P(("dp", "module"), None, None, None),
            P(("dp", "module")),
            P(),
            P("module", "dp", None),
        ),
        out_specs=P("dp", "module"),
        check_vma=False,
    )
```

```python
import functools

import jax
import jax.numpy as jnp
from jax import lax
from jax.experimental import pallas as pl
from jax.experimental.pallas import tpu as pltpu
from jax.sharding import PartitionSpec as P

ITERS = 4
NEAR = (2, -2, 1, -1)
FAR = 5
MESH = pl.DeviceIdType.MESH
BF16 = jnp.bfloat16
F32 = jnp.float32


def kernel(
    planes,
    slot_ref,
    len_ref,
    act_hbm,
    grad_hbm,
    query_ref,
    out_ref,
    act,
    grad,
    prod,
    tsend,
    tall,
    gpart,
    gcirc,
    gfull,
    gsend,
    near_in,
    far_out,
    far_in,
    qsrc,
    qfull,
    step_ref,
    resid_ref,
    acc_ref,
    ssend,
    srecv,
    slot_traces,
    plane_diags,
    diag_ref,
    load_sem,
    t_send,
    t_recv,
    tsib_send,
    tsib_recv,
    pair_send,
    pair_recv,
    q_send,
    q_recv,
    rs_send,
    rs_recv,
    g_send,
    g_recv,
    d_send,
    d_recv,
    tr_send,
    tr_recv,
    s_send,
    s_recv,
):
    per_dev, slots, rank, span = act.shape
    proj = rank * rank
    blocks = proj // 128
    kept = gcirc.shape[1]
    half = proj // 2
    band = half // planes
    rows = slots * per_dev
    queries = qfull.shape[1]
    per_owner = queries // slots
    assert planes == 16 and slots == 16
    examples = rows * 2 * planes

    dp, mod = lax.axis_index("dp"), lax.axis_index("module")
    z, y_lo = dp // 2, dp % 2
    core = mod % 2
    slot = (mod // 2) * 2 + y_lo

    def device(plane, chip, cc):
        return (plane * 2 + chip % 2, (chip // 2) * 2 + cc)

    way = 1 - 2 * core

    def along(count):
        return (z + 2 * planes + count) % planes

    def remote(src, dst, send, recv, target):
        return pltpu.make_async_remote_copy(
            src_ref=src, dst_ref=dst, send_sem=send, recv_sem=recv,
            device_id=target, device_id_type=MESH,
        )

    sibling = device(z, slot, 1 - core)

    def off(count):
        return device(along(count), slot, core)

    loads = [
        pltpu.make_async_copy(act_hbm, act, load_sem.at[0]),
        pltpu.make_async_copy(grad_hbm, grad, load_sem.at[1]),
    ]
    for load in loads:
        load.start()

    barrier = pltpu.get_barrier_semaphore()

    def greet(index, carry):
        chip, cc = index // 2, index % 2

        @pl.when(jnp.logical_or(chip != slot, cc != core))
        def _():
            pl.semaphore_signal(
                barrier, inc=1, device_id=device(z, chip, cc), device_id_type=MESH
            )

        return carry

    lax.fori_loop(0, 2 * slots, greet, 0)
    for count in NEAR + (3, -3, FAR, -FAR):
        pl.semaphore_signal(barrier, inc=1, device_id=off(count), device_id_type=MESH)
    qsrc[...] = query_ref[...].astype(BF16)

    for load in loads:
        load.wait()

    lanes = lax.broadcasted_iota(jnp.int32, (8, 4 * rank), 1) // rank
    positions = lax.broadcasted_iota(jnp.int32, (4 * rank, span), 1)

    def t_first(chip, cc):
        first = cc * rows + (chip % 2) * (rows // 2) + (chip // 2) * per_dev
        return pl.ds(pl.multiple_of(first, per_dev), per_dev)

    def t_rows(chip, cc):
        return tall.at[t_first(chip, cc), :]

    def holder(chip):
        found = jnp.int32(0)
        for index in range(slots):
            found = jnp.where(slot_ref[index] == chip, index, found)
        return found

    def project(first):
        held = [holder(first + r) for r in range(4)]
        for e in range(per_dev):
            left = jnp.concatenate([act[e, h] for h in held], axis=0)
            right = jnp.concatenate([grad[e, h] for h in held], axis=0)
            left = jnp.where(positions < len_ref[e], left, jnp.zeros_like(left))
            prod[pl.ds(e * 4 * rank, 4 * rank), :] = lax.dot_general(
                left, right, (((1,), (1,)), ((), ())), preferred_element_type=F32
            )
        for r in range(4):
            for g in range(proj // (4 * rank)):
                halves = []
                for h in range(per_dev // 8):
                    merged = None
                    for b in range(4):
                        row = h * 8 * 4 * rank + r * rank + 4 * g + b
                        piece = prod[pl.ds(row, 8, stride=4 * rank), :]
                        if b != r:
                            piece = pltpu.roll(piece, ((b - r) % 4) * rank, 1)
                        merged = piece if merged is None else jnp.where(lanes == b, piece, merged)
                    halves.append(merged)
                tsend[first + r, :, pl.ds(g * 4 * rank, 4 * rank)] = jnp.concatenate(
                    halves, axis=0
                ).astype(BF16)

    def t_to(chip):
        return remote(
            tsend.at[chip], t_rows(slot, core), t_send.at[chip], t_recv.at[slot],
            device(z, chip, core),
        )

    partner = device(z, (slot // 2) * 2 + core, y_lo)

    def q_part(plane):
        return qfull.at[pl.ds(pl.multiple_of((plane * 2 + core) * band, band), band), :]

    dp_rows = pl.ds(pl.multiple_of(dp * band, band), band)
    pair_out = remote(qsrc, qfull.at[dp_rows, :], pair_send.at[0], pair_recv.at[0], partner)
    pair_in = remote(q_part(z), q_part(z), pair_send.at[0], pair_recv.at[0], partner)

    def gather(part, send, recv, share):
        def carried(offset, count):
            block = part(along(offset))
            mark = (offset - count) % planes
            return remote(block, block, send.at[mark], recv.at[mark], off(count))

        def arrived(mark):
            block = part(along(mark))
            return remote(block, block, send.at[mark], recv.at[mark], sibling)

        def last():
            block = part(along(FAR * way))
            return remote(block, block, send.at[8], recv.at[8], off(-3 * way))

        def across(mark):
            block = part(along(mark))
            return remote(
                block, block, send.at[planes + mark], recv.at[planes + mark], sibling
            )

        def begin():
            for count in (FAR, -FAR) + NEAR:
                carried(0, count).start()
            if share:
                across(0).start()

        def go_on():
            for offset in (FAR, -FAR):
                arrived(offset % planes).wait_recv()
                for count in NEAR:
                    carried(offset, count).start()
            last().start()
            if share:
                across(FAR).start()
                across(planes - FAR).start()

        def finish():
            rest = [n % planes for n in (1, -1, 2, -2, 6, -6, 4, -4, 7, -7, 3, -3, 8)]
            for mark in rest:
                arrived(mark).wait_recv()
                if share:
                    across(mark).start()
            if share:
                for mark in [0, FAR, planes - FAR] + rest:
                    other = remote(
                        share(along(mark)), share(along(mark)), send.at[planes + mark],
                        recv.at[planes + mark], sibling,
                    )
                    other.wait_recv()
                    across(mark).wait_send()
            for count in (FAR, -FAR) + NEAR:
                carried(0, count).wait_send()
            for offset in (FAR, -FAR):
                for count in NEAR:
                    carried(offset, count).wait_send()
            last().wait_send()

        return begin, go_on, finish

    q_begin, q_go_on, q_finish = gather(
        q_part, q_send, q_recv,
        lambda plane: qfull.at[
            pl.ds(pl.multiple_of((plane * 2 + 1 - core) * band, band), band), :
        ],
    )
    d_begin, d_go_on, d_finish = gather(lambda plane: plane_diags.at[plane], d_send, d_recv, None)
    g_begin, g_go_on, g_finish = gather(
        lambda plane: gcirc.at[pl.ds(pl.multiple_of(core * half + plane * band, band), band), :],
        g_send, g_recv,
        lambda plane: gcirc.at[
            pl.ds(pl.multiple_of((1 - core) * half + plane * band, band), band), :
        ],
    )

    def first_of(k):
        return ((slot // 4 + 1 + k) % (slots // 4)) * 4

    def scatter(first):
        for r in range(4):

            @pl.when(first + r != slot)
            def _():
                t_to(first + r).start()

    project(first_of(0))
    pl.semaphore_wait(barrier, 2 * slots - 1 + 8)

    @pl.when(y_lo != core)
    def _():
        pair_out.start()

    @pl.when(y_lo == core)
    def _():
        qfull[dp_rows, :] = qsrc[...]

    scatter(first_of(0))

    def group(k, carry):
        project(first_of(k))
        scatter(first_of(k))

        @pl.when(k == 1)
        def _():
            pl.when(y_lo != core)(lambda: pair_in.wait_recv())
            q_begin()

        return carry

    lax.fori_loop(1, slots // 4, group, 0)
    tall[t_first(slot, core), :] = tsend[slot]

    def collect(k, carry):
        chip = ((slot // 4 + slots // 4 - 1 - k // 4) % (slots // 4)) * 4 + (slot + k) % 4

        @pl.when(chip != slot)
        def _():
            remote(
                t_rows(chip, core), t_rows(chip, core), t_send.at[chip], t_recv.at[chip], sibling
            ).wait_recv()

        remote(
            t_rows(chip, core), t_rows(chip, core), tsib_send.at[chip], tsib_recv.at[chip], sibling
        ).start()
        return carry

    lax.fori_loop(0, slots // 2, collect, 0)
    q_go_on()
    lax.fori_loop(slots // 2, slots, collect, 0)

    def collected(chip, carry):
        other = remote(
            t_rows(chip, 1 - core), t_rows(chip, 1 - core), tsib_send.at[chip], tsib_recv.at[chip],
            sibling,
        )
        other.wait_recv()
        other.wait_send()
        return carry

    lax.fori_loop(0, slots, collected, 0)

    apart = lax.broadcasted_iota(jnp.int32, (128, 128), 0) != lax.broadcasted_iota(
        jnp.int32, (128, 128), 1
    )
    per_block = 128 // band

    def columns(start, count):
        return tall[:, pl.ds(pl.multiple_of(start, 128), count)]

    def store(n, offset, value):
        for q in range(per_block):
            piece = value[q * band : (q + 1) * band]
            gpart[n * per_block + q, :, pl.ds(offset, value.shape[1])] = piece
            gsend[n * per_block + q, :, pl.ds(offset, value.shape[1])] = piece.astype(BF16)

    for n in range(half // 128):
        first = core * half + n * 128
        left = columns(first, 128)
        direct = half - n * 128
        value = lax.dot_general(
            left, columns(first, direct), (((0,), (0,)), ((), ())), preferred_element_type=F32
        )
        store(n, 0, jnp.where(apart, value[:, :128], 0.0))
        if direct > 128:
            store(n, 128, value[:, 128:])
        value = lax.dot_general(
            left, columns((1 - core) * half, kept - direct), (((0,), (0,)), ((), ())),
            preferred_element_type=F32,
        )
        store(n, direct, value)

    def near_send(count, a):
        index = NEAR.index(count) * 3 + a + 1
        return remote(
            gsend.at[along(count - FAR * a)], near_in.at[index], rs_send.at[index],
            rs_recv.at[index], off(count),
        )

    extra = 3 * len(NEAR)
    last_send = remote(
        gsend.at[along(8)], near_in.at[extra], rs_send.at[extra], rs_recv.at[extra], off(-3 * way)
    )

    def far_send(a):
        index = extra + 1 + (a + 1) // 2
        return remote(
            far_out.at[(a + 1) // 2], far_in.at[(a + 1) // 2], rs_send.at[index],
            rs_recv.at[index], off(-FAR * a),
        )

    for count in NEAR:
        for a in (1, -1):
            near_send(count, a).start()
    last_send.start()
    for count in NEAR:
        near_send(count, 0).start()

    squares = tall[...].astype(F32)
    squares = jnp.sum(squares * squares, axis=0, keepdims=True)
    for n in range(blocks):
        plane_diags[z, pl.ds(n, 1), :] = squares[:, n * 128 : (n + 1) * 128]
    d_begin()

    def window(a):
        value = gpart[along(-FAR * a)]
        for count in NEAR:
            near_send(count, a).wait_recv()
            value = value + near_in[NEAR.index(count) * 3 + a + 1].astype(F32)
        return value

    upward, downward = window(1), window(-1)
    last_send.wait_recv()
    more = near_in[extra].astype(F32)
    far_out[1] = (upward + jnp.where(core == 0, more, 0.0)).astype(BF16)
    far_send(1).start()
    far_out[0] = (downward + jnp.where(core == 0, 0.0, more)).astype(BF16)
    far_send(-1).start()
    d_go_on()
    value = window(0)
    d_finish()

    diagonal = jnp.sum(plane_diags[...], axis=0) / examples
    own_eig = jnp.sum(jnp.sum(diagonal, axis=1, keepdims=True), axis=0, keepdims=True) / proj
    slot_traces[slot] = jnp.broadcast_to(own_eig, (8, 128))
    diag_ref[...] = jnp.concatenate([diagonal[n : n + 1] for n in range(blocks)], axis=1)

    def trace_to(chip):
        return remote(
            slot_traces.at[slot], slot_traces.at[slot], tr_send.at[chip], tr_recv.at[slot],
            device(z, chip, core),
        )

    def trace_from(chip):
        return remote(
            slot_traces.at[chip], slot_traces.at[chip], tr_send.at[chip], tr_recv.at[chip], sibling
        )

    def tell(k, carry):
        trace_to((slot + k) % slots).start()
        return carry

    for a in (1, -1):
        far_send(a).wait_recv()
        value = value + far_in[(a + 1) // 2].astype(F32)
    gcirc[pl.ds(pl.multiple_of(core * half + z * band, band), band), :] = value.astype(BF16)
    g_begin()
    lax.fori_loop(1, slots, tell, 0)

    def settle(k, carry):
        chip = (slot + k) % slots
        t_to(chip).wait_send()
        trace_to(chip).wait_send()
        trace_from(chip).wait_recv()
        return carry

    lax.fori_loop(1, slots, settle, 0)
    pl.when(y_lo != core)(lambda: pair_out.wait_send())
    for count in NEAR:
        for a in (1, -1, 0):
            near_send(count, a).wait_send()
    last_send.wait_send()
    for a in (1, -1):
        far_send(a).wait_send()
    g_go_on()
    q_finish()
    g_finish()

    for n in range(blocks):
        for k in range(kept // 128):
            piece = gcirc[n * 128 : (n + 1) * 128, k * 128 : (k + 1) * 128]
            other = (n + k) % blocks
            gfull[n * 128 : (n + 1) * 128, other * 128 : (other + 1) * 128] = piece
            if 0 < k < blocks - k:
                gfull[other * 128 : (other + 1) * 128, n * 128 : (n + 1) * 128] = piece.T

    damping = 0.1 * (jnp.sum(slot_traces[...], axis=0)[0:1, 0:1] / slots)
    upper = damping + 4.0 * own_eig
    center = (upper + damping) / 2.0
    radius = (upper - damping) / 2.0
    sigma = center / radius
    rho = 1.0 / sigma
    train = tall[pl.ds(pl.multiple_of(core * rows, rows), rows), :].astype(F32)
    resid_ref[...] = train
    step_ref[...] = train / center
    acc_ref[...] = step_ref[...]
    tile = min(256, proj)
    for index in range(ITERS - 1):
        rho_next = 1.0 / (2.0 * sigma - rho)
        rounded = step_ref[...].astype(BF16)

        def column(n, carry):
            cols = pl.ds(pl.multiple_of(n * tile, tile), tile)
            product = jnp.dot(rounded, gfull[:, cols], preferred_element_type=F32)
            step = step_ref[:, cols]
            resid = resid_ref[:, cols] - (
                product * (1.0 / examples) + (diag_ref[:, cols] + damping) * step
            )
            resid_ref[:, cols] = resid
            step = rho_next * rho * step + (2.0 * rho_next / radius) * resid
            step_ref[:, cols] = step
            acc_ref[:, cols] = acc_ref[:, cols] + step
            return carry

        lax.fori_loop(0, proj // tile, column, 0)
        rho = rho_next

    scores = jnp.dot(acc_ref[...].astype(BF16), qfull[...], preferred_element_type=F32)
    ssend[...] = scores.T.astype(BF16)

    def block(index):
        owner, low = index // 2, index % 2
        return ssend.at[
            pl.ds(pl.multiple_of(owner * per_owner, per_owner), per_owner),
            pl.ds(pl.multiple_of(low * (rows // 2), rows // 2), rows // 2),
        ]

    mark = slot * 2 + core

    def score_to(index):
        return remote(
            block(index), srecv.at[mark], s_send.at[index], s_recv.at[mark],
            (z * 2 + index % 2, index // 2),
        )

    own = mod * 2 + y_lo

    def push(k, carry):
        index = (own + k) % (2 * slots)
        score_to(index).start()
        return carry

    lax.fori_loop(1, 2 * slots, push, 0)
    srecv[mark] = ssend[
        pl.ds(pl.multiple_of(mod * per_owner, per_owner), per_owner),
        pl.ds(pl.multiple_of(y_lo * (rows // 2), rows // 2), rows // 2),
    ]

    def pull(k, carry):
        index = (mark + k) % (2 * slots)
        remote(
            srecv.at[index], srecv.at[index], s_send.at[index], s_recv.at[index], sibling
        ).wait_recv()
        return carry

    lax.fori_loop(1, 2 * slots, pull, 0)
    sums = []
    for cc in range(2):
        summed = srecv[cc].astype(F32)
        for chip in range(1, slots):
            summed = summed + srecv[chip * 2 + cc].astype(F32)
        sums.append(summed)
    width = rows // 2
    runs = width // per_dev
    lane_run = lax.broadcasted_iota(jnp.int32, (per_owner, width), 1) // per_dev
    for h in range(2):
        merged = jnp.zeros((per_owner, width), F32)
        for n in range(runs // 2):
            for cc in range(2):
                shift = (2 * n + cc - (h * (runs // 2) + n)) % runs
                piece = pltpu.roll(sums[cc], shift * per_dev, 1) if shift else sums[cc]
                merged = jnp.where(lane_run == 2 * n + cc, piece, merged)
        out_ref[:, pl.ds(h * width, width)] = merged

    def pushed(k, carry):
        score_to((own + k) % (2 * slots)).wait_send()
        return carry

    lax.fori_loop(1, 2 * slots, pushed, 0)


def per_device(planes, act_factors, grad_factors, lengths, module_slot, query_grads):
    per_dev, slots, rank, span = act_factors.shape
    proj = rank * rank
    rows = slots * per_dev
    band, queries = query_grads.shape[1:]
    per_owner = queries // slots
    kept = (proj // 128 // 2 + 1) * 128
    sem = pltpu.SemaphoreType.DMA
    vmem = pltpu.VMEM
    result = pl.pallas_call(
        functools.partial(kernel, planes),
        out_shape=jax.ShapeDtypeStruct((per_owner, rows), F32),
        in_specs=[
            pl.BlockSpec(memory_space=pltpu.SMEM),
            pl.BlockSpec(memory_space=pltpu.SMEM),
            pl.BlockSpec(memory_space=pltpu.HBM),
            pl.BlockSpec(memory_space=pltpu.HBM),
            pl.BlockSpec(memory_space=pltpu.VMEM),
        ],
        out_specs=pl.BlockSpec(memory_space=pltpu.VMEM),
        scratch_shapes=[
            vmem((per_dev, slots, rank, span), BF16),
            vmem((per_dev, slots, rank, span), BF16),
            vmem((per_dev * 4 * rank, 4 * rank), F32),
            vmem((slots, per_dev, proj), BF16),
            vmem((2 * rows, proj), BF16),
            vmem((planes, band, kept), F32),
            vmem((proj, kept), BF16),
            vmem((proj, proj), BF16),
            vmem((planes, band, kept), BF16),
            vmem((13, band, kept), BF16),
            vmem((2, band, kept), BF16),
            vmem((2, band, kept), BF16),
            vmem((band, queries), BF16),
            vmem((proj, queries), BF16),
            vmem((rows, proj), F32),
            vmem((rows, proj), F32),
            vmem((rows, proj), F32),
            vmem((queries, rows), BF16),
            vmem((2 * slots, per_owner, rows // 2), BF16),
            vmem((slots, 8, 128), F32),
            vmem((planes, proj // 128, 128), F32),
            vmem((1, proj), F32),
            sem((2,)),
            sem((slots,)),
            sem((slots,)),
            sem((slots,)),
            sem((slots,)),
            sem((1,)),
            sem((1,)),
            sem((2 * planes,)),
            sem((2 * planes,)),
            sem((15,)),
            sem((15,)),
            sem((2 * planes,)),
            sem((2 * planes,)),
            sem((planes,)),
            sem((planes,)),
            sem((slots,)),
            sem((slots,)),
            sem((2 * slots,)),
            sem((2 * slots,)),
        ],
        compiler_params=pltpu.CompilerParams(
            collective_id=0, has_side_effects=True, vmem_limit_bytes=62 * 1024 * 1024
        ),
    )(module_slot, lengths, act_factors, grad_factors, query_grads[0])
    return result.T


def solution(mesh):
    planes = mesh.shape["dp"] // 2
    return jax.shard_map(
        functools.partial(per_device, planes),
        mesh=mesh,
        in_specs=(
            P(("dp", "module"), None, None, None),
            P(("dp", "module"), None, None, None),
            P(("dp", "module")),
            P(),
            P("module", "dp", None),
        ),
        out_specs=P("dp", "module"),
        check_vma=False,
    )
```

```python
import functools

import jax
import jax.numpy as jnp
from jax import lax
from jax.experimental import pallas as pl
from jax.experimental.pallas import tpu as pltpu
from jax.sharding import PartitionSpec as P

ITERS = 4
NEAR = (2, -2, 1, -1)
FAR = 5
LOADS = 4
MESH = pl.DeviceIdType.MESH
BF16 = jnp.bfloat16
F32 = jnp.float32


def kernel(
    planes,
    slot_ref,
    len_ref,
    act_hbm,
    grad_hbm,
    query_ref,
    out_ref,
    act,
    grad,
    prod,
    tsend,
    tall,
    gpart,
    gcirc,
    gfull,
    gsend,
    near_in,
    far_out,
    far_in,
    qsrc,
    qfull,
    step_ref,
    resid_ref,
    acc_ref,
    ssend,
    srecv,
    slot_traces,
    plane_diags,
    diag_ref,
    load_sem,
    t_send,
    t_recv,
    tsib_send,
    tsib_recv,
    q_send,
    q_recv,
    rs_send,
    rs_recv,
    g_send,
    g_recv,
    d_send,
    d_recv,
    tr_send,
    tr_recv,
    s_send,
    s_recv,
):
    per_dev, slots, rank, span = act.shape
    proj = rank * rank
    blocks = proj // 128
    kept = gcirc.shape[1]
    half = proj // 2
    band = half // planes
    rows = slots * per_dev
    queries = qfull.shape[1]
    per_owner = queries // slots
    assert planes == 16 and slots == 16
    examples = rows * 2 * planes

    dp, mod = lax.axis_index("dp"), lax.axis_index("module")
    z, y_lo = dp // 2, dp % 2
    core = mod % 2
    slot = (mod // 2) * 2 + y_lo

    def device(plane, chip, cc):
        return (plane * 2 + chip % 2, (chip // 2) * 2 + cc)

    way = 1 - 2 * core

    def along(count):
        return (z + 2 * planes + count) % planes

    def remote(src, dst, send, recv, target):
        return pltpu.make_async_remote_copy(
            src_ref=src, dst_ref=dst, send_sem=send, recv_sem=recv,
            device_id=target, device_id_type=MESH,
        )

    sibling = device(z, slot, 1 - core)

    def off(count):
        return device(along(count), slot, core)

    def twin(count):
        return device(along(count), (slot // 2) * 2 + core, y_lo)

    barrier = pltpu.get_barrier_semaphore()
    for count in (FAR, -FAR, 3, -3) + NEAR:
        pl.semaphore_signal(barrier, inc=1, device_id=off(count), device_id_type=MESH)
    for count in (FAR, -FAR) + NEAR:
        pl.semaphore_signal(barrier, inc=1, device_id=twin(count), device_id_type=MESH)

    def greet(index, carry):
        chip, cc = index // 2, index % 2

        @pl.when(jnp.logical_or(chip != slot, cc != core))
        def _():
            pl.semaphore_signal(
                barrier, inc=1, device_id=device(z, chip, cc), device_id_type=MESH
            )

        return carry

    lax.fori_loop(0, 2 * slots, greet, 0)
    part = per_dev // LOADS
    loads = [
        pltpu.make_async_copy(
            whole.at[pl.ds(n * part, part)], held.at[pl.ds(n * part, part)], load_sem.at[n, side]
        )
        for n in range(LOADS)
        for side, (whole, held) in enumerate(((act_hbm, act), (grad_hbm, grad)))
    ]
    for load in loads:
        load.start()

    qsrc[...] = query_ref[...].astype(BF16)

    for load in loads:
        load.wait()

    lanes = lax.broadcasted_iota(jnp.int32, (8, 4 * rank), 1) // rank
    positions = lax.broadcasted_iota(jnp.int32, (4 * rank, span), 1)

    def t_first(chip, cc):
        first = cc * rows + (chip % 2) * (rows // 2) + (chip // 2) * per_dev
        return pl.ds(pl.multiple_of(first, per_dev), per_dev)

    def t_rows(chip, cc):
        return tall.at[t_first(chip, cc), :]

    def holder(chip):
        found = jnp.int32(0)
        for index in range(slots):
            found = jnp.where(slot_ref[index] == chip, index, found)
        return found

    pitch = prod.shape[0] // per_dev

    def project(chips):
        held = [holder(chip) for chip in chips]
        for e in range(per_dev):
            left = jnp.concatenate([act[e, h] for h in held], axis=0)
            right = jnp.concatenate([grad[e, h] for h in held], axis=0)
            left = jnp.where(positions < len_ref[e], left, jnp.zeros_like(left))
            prod[pl.ds(e * pitch, 4 * rank), :] = lax.dot_general(
                left, right, (((1,), (1,)), ((), ())), preferred_element_type=F32
            )
        for r in range(4):
            for g in range(proj // (4 * rank)):
                halves = []
                for h in range(per_dev // 8):
                    merged = None
                    for b in range(4):
                        row = h * 8 * pitch + r * rank + 4 * g + b
                        piece = prod[pl.ds(row, 8, stride=pitch), :]
                        if b != r:
                            piece = pltpu.roll(piece, ((b - r) % 4) * rank, 1)
                        merged = piece if merged is None else jnp.where(lanes == b, piece, merged)
                    halves.append(merged)
                tsend[chips[r], :, pl.ds(g * 4 * rank, 4 * rank)] = jnp.concatenate(
                    halves, axis=0
                ).astype(BF16)

    def t_to(chip):
        return remote(
            tsend.at[chip], t_rows(slot, core), t_send.at[chip], t_recv.at[slot],
            device(z, chip, core),
        )

    def q_part(plane):
        return qfull.at[pl.ds(pl.multiple_of((plane * 2 + core) * band, band), band), :]

    dp_rows = pl.ds(pl.multiple_of(dp * band, band), band)

    def q_first(count):
        mark = -count % planes
        return remote(qsrc, qfull.at[dp_rows, :], q_send.at[mark], q_recv.at[mark], twin(count))

    q_home = remote(q_part(z), q_part(z), q_send.at[0], q_recv.at[0], sibling)

    def gather(part, send, recv, share):
        def carried(offset, count):
            block = part(along(offset))
            mark = (offset - count) % planes
            return remote(block, block, send.at[mark], recv.at[mark], off(count))

        def arrived(mark):
            block = part(along(mark))
            return remote(block, block, send.at[mark], recv.at[mark], sibling)

        def last():
            block = part(along(FAR * way))
            return remote(block, block, send.at[8], recv.at[8], off(-3 * way))

        def across(mark):
            block = part(along(mark))
            return remote(
                block, block, send.at[planes + mark], recv.at[planes + mark], sibling
            )

        def begin():
            for count in (FAR, -FAR) + NEAR:
                carried(0, count).start()

        def go_on():
            for offset in (FAR, -FAR):
                arrived(offset % planes).wait_recv()
                for count in NEAR:
                    carried(offset, count).start()
            last().start()
            if share:
                for mark in (0, FAR, planes - FAR):
                    across(mark).start()

        def finish():
            rest = [n % planes for n in (1, -1, 2, -2, 6, -6, 4, -4, 7, -7, 3, -3, 8)]
            for mark in rest:
                arrived(mark).wait_recv()
                if share:
                    across(mark).start()
            if share:
                for mark in [0, FAR, planes - FAR] + rest:
                    other = remote(
                        share(along(mark)), share(along(mark)), send.at[planes + mark],
                        recv.at[planes + mark], sibling,
                    )
                    other.wait_recv()
                    across(mark).wait_send()
            for count in (FAR, -FAR) + NEAR:
                carried(0, count).wait_send()
            for offset in (FAR, -FAR):
                for count in NEAR:
                    carried(offset, count).wait_send()
            last().wait_send()

        return begin, go_on, finish

    _, q_go_on, q_finish = gather(
        q_part, q_send, q_recv,
        lambda plane: qfull.at[
            pl.ds(pl.multiple_of((plane * 2 + 1 - core) * band, band), band), :
        ],
    )
    d_begin, d_go_on, d_finish = gather(lambda plane: plane_diags.at[plane], d_send, d_recv, None)
    g_begin, g_go_on, g_finish = gather(
        lambda plane: gcirc.at[pl.ds(pl.multiple_of(core * half + plane * band, band), band), :],
        g_send, g_recv,
        lambda plane: gcirc.at[
            pl.ds(pl.multiple_of((1 - core) * half + plane * band, band), band), :
        ],
    )

    def chips_of(k, sign):
        chips = []
        for r in range(4):
            x, y = (slot // 4 + 4 + sign * r) % 4, (slot + 4 + sign * ((r + k) % 4)) % 4
            chips.append(x * 4 + y)
        return chips

    def scatter(chips):
        for r in (2, 1, 3, 0):

            @pl.when(chips[r] != slot)
            def _():
                t_to(chips[r]).start()

    def group(k, carry):
        project(chips_of(k, 1))
        return carry

    lax.fori_loop(1, slots // 4 + 1, group, 0)
    pl.semaphore_wait(barrier, 2 * slots - 1 + 14)

    def spread(k, carry):
        scatter(chips_of(k, 1))
        return carry

    lax.fori_loop(1, slots // 4 + 1, spread, 0)
    for count in (FAR, -FAR) + NEAR:
        q_first(count).start()

    @pl.when(y_lo != core)
    def _():
        q_first(0).start()

    @pl.when(y_lo == core)
    def _():
        qfull[dp_rows, :] = qsrc[...]

    tall[t_first(slot, core), :] = tsend[slot]

    def collect(k, carry):
        chips = chips_of(k, -1)
        for r in (1, 3, 2, 0):
            chip = chips[r]

            @pl.when(chip != slot)
            def _():
                remote(
                    t_rows(chip, core), t_rows(chip, core), t_send.at[chip], t_recv.at[chip],
                    sibling,
                ).wait_recv()

            remote(
                t_rows(chip, core), t_rows(chip, core), tsib_send.at[chip], tsib_recv.at[chip],
                sibling,
            ).start()
        return carry

    lax.fori_loop(1, 3, collect, 0)
    pl.when(y_lo != core)(lambda: q_home.wait_recv())
    q_go_on()
    lax.fori_loop(3, slots // 4 + 1, collect, 0)

    def collected(chip, carry):
        other = remote(
            t_rows(chip, 1 - core), t_rows(chip, 1 - core), tsib_send.at[chip], tsib_recv.at[chip],
            sibling,
        )
        other.wait_recv()
        other.wait_send()
        return carry

    lax.fori_loop(0, slots, collected, 0)

    apart = lax.broadcasted_iota(jnp.int32, (128, 128), 0) != lax.broadcasted_iota(
        jnp.int32, (128, 128), 1
    )
    per_block = 128 // band

    def columns(start, count):
        return tall[:, pl.ds(pl.multiple_of(start, 128), count)]

    def store(n, offset, value):
        for q in range(per_block):
            piece = value[q * band : (q + 1) * band]
            gpart[n * per_block + q, :, pl.ds(offset, value.shape[1])] = piece
            gsend[n * per_block + q, :, pl.ds(offset, value.shape[1])] = piece.astype(BF16)

    for n in range(half // 128):
        first = core * half + n * 128
        left = columns(first, 128)
        direct = half - n * 128
        value = lax.dot_general(
            left, columns(first, direct), (((0,), (0,)), ((), ())), preferred_element_type=F32
        )
        store(n, 0, jnp.where(apart, value[:, :128], 0.0))
        if direct > 128:
            store(n, 128, value[:, 128:])
        value = lax.dot_general(
            left, columns((1 - core) * half, kept - direct), (((0,), (0,)), ((), ())),
            preferred_element_type=F32,
        )
        store(n, direct, value)

    def near_send(count, a):
        index = NEAR.index(count) * 3 + a + 1
        return remote(
            gsend.at[along(count - FAR * a)], near_in.at[index], rs_send.at[index],
            rs_recv.at[index], off(count),
        )

    extra = 3 * len(NEAR)
    last_send = remote(
        gsend.at[along(8)], near_in.at[extra], rs_send.at[extra], rs_recv.at[extra], off(-3 * way)
    )

    def far_send(a):
        index = extra + 1 + (a + 1) // 2
        return remote(
            far_out.at[(a + 1) // 2], far_in.at[(a + 1) // 2], rs_send.at[index],
            rs_recv.at[index], off(-FAR * a),
        )

    for count in NEAR:
        for a in (1, -1):
            near_send(count, a).start()
    last_send.start()

    squares = tall[...].astype(F32)
    squares = jnp.sum(squares * squares, axis=0, keepdims=True)
    for n in range(blocks):
        plane_diags[z, pl.ds(n, 1), :] = squares[:, n * 128 : (n + 1) * 128]
    d_begin()

    def window(a):
        value = gpart[along(-FAR * a)]
        for count in NEAR:
            near_send(count, a).wait_recv()
            value = value + near_in[NEAR.index(count) * 3 + a + 1].astype(F32)
        return value

    upward, downward = window(1), window(-1)
    last_send.wait_recv()
    more = near_in[extra].astype(F32)
    far_out[1] = (upward + jnp.where(core == 0, more, 0.0)).astype(BF16)
    far_send(1).start()
    far_out[0] = (downward + jnp.where(core == 0, 0.0, more)).astype(BF16)
    far_send(-1).start()
    for count in NEAR:
        near_send(count, 0).start()
    d_go_on()
    value = window(0)

    for a in (1, -1):
        far_send(a).wait_recv()
        value = value + far_in[(a + 1) // 2].astype(F32)
    gcirc[pl.ds(pl.multiple_of(core * half + z * band, band), band), :] = value.astype(BF16)
    g_begin()

    d_finish()
    diagonal = jnp.sum(plane_diags[...], axis=0) / examples
    own_eig = jnp.sum(jnp.sum(diagonal, axis=1, keepdims=True), axis=0, keepdims=True) / proj
    slot_traces[slot] = jnp.broadcast_to(own_eig, (8, 128))
    diag_ref[...] = jnp.concatenate([diagonal[n : n + 1] for n in range(blocks)], axis=1)

    def trace_to(chip):
        return remote(
            slot_traces.at[slot], slot_traces.at[slot], tr_send.at[chip], tr_recv.at[slot],
            device(z, chip, core),
        )

    def trace_from(chip):
        return remote(
            slot_traces.at[chip], slot_traces.at[chip], tr_send.at[chip], tr_recv.at[chip], sibling
        )

    def tell(k, carry):
        trace_to((slot + k) % slots).start()
        return carry

    lax.fori_loop(1, slots, tell, 0)
    g_go_on()

    def settle(k, carry):
        chip = (slot + k) % slots
        t_to(chip).wait_send()
        trace_to(chip).wait_send()
        trace_from(chip).wait_recv()
        return carry

    lax.fori_loop(1, slots, settle, 0)
    pl.when(y_lo != core)(lambda: q_first(0).wait_send())
    for count in NEAR:
        for a in (1, -1, 0):
            near_send(count, a).wait_send()
    last_send.wait_send()
    for a in (1, -1):
        far_send(a).wait_send()
    q_finish()
    g_finish()

    for n in range(blocks):
        for k in range(kept // 128):
            piece = gcirc[n * 128 : (n + 1) * 128, k * 128 : (k + 1) * 128]
            other = (n + k) % blocks
            gfull[n * 128 : (n + 1) * 128, other * 128 : (other + 1) * 128] = piece
            if 0 < k < blocks - k:
                gfull[other * 128 : (other + 1) * 128, n * 128 : (n + 1) * 128] = piece.T

    damping = 0.1 * (jnp.sum(slot_traces[...], axis=0)[0:1, 0:1] / slots)
    upper = damping + 4.0 * own_eig
    center = (upper + damping) / 2.0
    radius = (upper - damping) / 2.0
    sigma = center / radius
    rho = 1.0 / sigma
    train = tall[pl.ds(pl.multiple_of(core * rows, rows), rows), :].astype(F32)
    resid_ref[...] = train
    step_ref[...] = train / center
    acc_ref[...] = step_ref[...]
    tile = min(256, proj)
    for index in range(ITERS - 1):
        rho_next = 1.0 / (2.0 * sigma - rho)
        rounded = step_ref[...].astype(BF16)

        for n in range(proj // tile):
            cols = pl.ds(n * tile, tile)
            product = jnp.dot(rounded, gfull[:, cols], preferred_element_type=F32)
            step = step_ref[:, cols]
            resid = resid_ref[:, cols] - (
                product * (1.0 / examples) + (diag_ref[:, cols] + damping) * step
            )
            resid_ref[:, cols] = resid
            step = rho_next * rho * step + (2.0 * rho_next / radius) * resid
            step_ref[:, cols] = step
            acc_ref[:, cols] = acc_ref[:, cols] + step
        rho = rho_next

    scores = jnp.dot(acc_ref[...].astype(BF16), qfull[...], preferred_element_type=F32)
    ssend[...] = scores.T.astype(BF16)

    def block(index):
        owner, low = index // 2, index % 2
        return ssend.at[
            pl.ds(pl.multiple_of(owner * per_owner, per_owner), per_owner),
            pl.ds(pl.multiple_of(low * (rows // 2), rows // 2), rows // 2),
        ]

    mark = slot * 2 + core

    def score_to(index):
        return remote(
            block(index), srecv.at[mark], s_send.at[index], s_recv.at[mark],
            (z * 2 + index % 2, index // 2),
        )

    own = mod * 2 + y_lo

    def push(k, carry):
        index = (own + k) % (2 * slots)
        score_to(index).start()
        return carry

    lax.fori_loop(1, 2 * slots, push, 0)
    srecv[mark] = ssend[
        pl.ds(pl.multiple_of(mod * per_owner, per_owner), per_owner),
        pl.ds(pl.multiple_of(y_lo * (rows // 2), rows // 2), rows // 2),
    ]

    def pull(k, carry):
        index = (mark + k) % (2 * slots)
        remote(
            srecv.at[index], srecv.at[index], s_send.at[index], s_recv.at[index], sibling
        ).wait_recv()
        return carry

    lax.fori_loop(1, 2 * slots, pull, 0)
    sums = []
    for cc in range(2):
        summed = srecv[cc].astype(F32)
        for chip in range(1, slots):
            summed = summed + srecv[chip * 2 + cc].astype(F32)
        sums.append(summed)
    width = rows // 2
    runs = width // per_dev
    lane_run = lax.broadcasted_iota(jnp.int32, (per_owner, width), 1) // per_dev
    for h in range(2):
        merged = jnp.zeros((per_owner, width), F32)
        for n in range(runs // 2):
            for cc in range(2):
                shift = (2 * n + cc - (h * (runs // 2) + n)) % runs
                piece = pltpu.roll(sums[cc], shift * per_dev, 1) if shift else sums[cc]
                merged = jnp.where(lane_run == 2 * n + cc, piece, merged)
        out_ref[:, pl.ds(h * width, width)] = merged

    def pushed(k, carry):
        score_to((own + k) % (2 * slots)).wait_send()
        return carry

    lax.fori_loop(1, 2 * slots, pushed, 0)


def per_device(planes, act_factors, grad_factors, lengths, module_slot, query_grads):
    per_dev, slots, rank, span = act_factors.shape
    proj = rank * rank
    rows = slots * per_dev
    band, queries = query_grads.shape[1:]
    per_owner = queries // slots
    kept = (proj // 128 // 2 + 1) * 128
    sem = pltpu.SemaphoreType.DMA
    vmem = pltpu.VMEM
    result = pl.pallas_call(
        functools.partial(kernel, planes),
        out_shape=jax.ShapeDtypeStruct((per_owner, rows), F32),
        in_specs=[
            pl.BlockSpec(memory_space=pltpu.SMEM),
            pl.BlockSpec(memory_space=pltpu.SMEM),
            pl.BlockSpec(memory_space=pltpu.HBM),
            pl.BlockSpec(memory_space=pltpu.HBM),
            pl.BlockSpec(memory_space=pltpu.VMEM),
        ],
        out_specs=pl.BlockSpec(memory_space=pltpu.VMEM),
        scratch_shapes=[
            vmem((per_dev, slots, rank, span), BF16),
            vmem((per_dev, slots, rank, span), BF16),
            vmem((per_dev * (4 * rank + 8), 4 * rank), F32),
            vmem((slots, per_dev, proj), BF16),
            vmem((2 * rows, proj), BF16),
            vmem((planes, band, kept), F32),
            vmem((proj, kept), BF16),
            vmem((proj, proj), BF16),
            vmem((planes, band, kept), BF16),
            vmem((13, band, kept), BF16),
            vmem((2, band, kept), BF16),
            vmem((2, band, kept), BF16),
            vmem((band, queries), BF16),
            vmem((proj, queries), BF16),
            vmem((rows, proj), F32),
            vmem((rows, proj), F32),
            vmem((rows, proj), F32),
            vmem((queries, rows), BF16),
            vmem((2 * slots, per_owner, rows // 2), BF16),
            vmem((slots, 8, 128), F32),
            vmem((planes, proj // 128, 128), F32),
            vmem((1, proj), F32),
            sem((LOADS, 2)),
            sem((slots,)),
            sem((slots,)),
            sem((slots,)),
            sem((slots,)),
            sem((2 * planes,)),
            sem((2 * planes,)),
            sem((15,)),
            sem((15,)),
            sem((2 * planes,)),
            sem((2 * planes,)),
            sem((planes,)),
            sem((planes,)),
            sem((slots,)),
            sem((slots,)),
            sem((2 * slots,)),
            sem((2 * slots,)),
        ],
        compiler_params=pltpu.CompilerParams(
            collective_id=0, has_side_effects=True, vmem_limit_bytes=62 * 1024 * 1024
        ),
    )(module_slot, lengths, act_factors, grad_factors, query_grads[0])
    return result.T


def solution(mesh):
    planes = mesh.shape["dp"] // 2
    return jax.shard_map(
        functools.partial(per_device, planes),
        mesh=mesh,
        in_specs=(
            P(("dp", "module"), None, None, None),
            P(("dp", "module"), None, None, None),
            P(("dp", "module")),
            P(),
            P("module", "dp", None),
        ),
        out_specs=P("dp", "module"),
        check_vma=False,
    )
```

```python
import functools

import jax
import jax.numpy as jnp
from jax import lax
from jax.experimental import pallas as pl
from jax.experimental.pallas import tpu as pltpu
from jax.sharding import PartitionSpec as P

ITERS = 4
NEAR = (2, -2, 1, -1)
FAR = 5
LOADS = 4
MESH = pl.DeviceIdType.MESH
BF16 = jnp.bfloat16
F32 = jnp.float32


def kernel(
    planes,
    slot_ref,
    len_ref,
    act_hbm,
    grad_hbm,
    query_ref,
    out_ref,
    act,
    grad,
    prod,
    tsend,
    tall,
    gpart,
    gcirc,
    gfull,
    gsend,
    near_in,
    far_out,
    far_in,
    qsrc,
    qfull,
    step_ref,
    resid_ref,
    acc_ref,
    ssend,
    srecv,
    slot_traces,
    plane_diags,
    diag_ref,
    load_sem,
    t_send,
    t_recv,
    tsib_send,
    tsib_recv,
    q_send,
    q_recv,
    rs_send,
    rs_recv,
    g_send,
    g_recv,
    d_send,
    d_recv,
    tr_send,
    tr_recv,
    s_send,
    s_recv,
):
    per_dev, slots, rank, span = act.shape
    proj = rank * rank
    blocks = proj // 128
    kept = gcirc.shape[1]
    half = proj // 2
    band = half // planes
    rows = slots * per_dev
    queries = qfull.shape[1]
    per_owner = queries // slots
    assert planes == 16 and slots == 16
    examples = rows * 2 * planes

    dp, mod = lax.axis_index("dp"), lax.axis_index("module")
    z, y_lo = dp // 2, dp % 2
    core = mod % 2
    slot = (mod // 2) * 2 + y_lo

    def device(plane, chip, cc):
        return (plane * 2 + chip % 2, (chip // 2) * 2 + cc)

    way = 1 - 2 * core

    def along(count):
        return (z + 2 * planes + count) % planes

    def remote(src, dst, send, recv, target):
        return pltpu.make_async_remote_copy(
            src_ref=src, dst_ref=dst, send_sem=send, recv_sem=recv,
            device_id=target, device_id_type=MESH,
        )

    sibling = device(z, slot, 1 - core)

    def off(count):
        return device(along(count), slot, core)

    def twin(count):
        return device(along(count), (slot // 2) * 2 + core, y_lo)

    barrier = pltpu.get_barrier_semaphore()
    for count in (FAR, -FAR, 3, -3) + NEAR:
        pl.semaphore_signal(barrier, inc=1, device_id=off(count), device_id_type=MESH)
    for count in (FAR, -FAR) + NEAR:
        pl.semaphore_signal(barrier, inc=1, device_id=twin(count), device_id_type=MESH)

    def greet(index, carry):
        chip, cc = index // 2, index % 2

        @pl.when(jnp.logical_or(chip != slot, cc != core))
        def _():
            pl.semaphore_signal(
                barrier, inc=1, device_id=device(z, chip, cc), device_id_type=MESH
            )

        return carry

    lax.fori_loop(0, 2 * slots, greet, 0)
    part = per_dev // LOADS
    loads = [
        pltpu.make_async_copy(
            whole.at[pl.ds(n * part, part)], held.at[pl.ds(n * part, part)], load_sem.at[n, side]
        )
        for n in range(LOADS)
        for side, (whole, held) in enumerate(((act_hbm, act), (grad_hbm, grad)))
    ]
    for load in loads:
        load.start()

    qsrc[...] = query_ref[...].astype(BF16)

    for load in loads:
        load.wait()

    lanes = lax.broadcasted_iota(jnp.int32, (8, 4 * rank), 1) // rank
    positions = lax.broadcasted_iota(jnp.int32, (4 * rank, span), 1)

    def t_first(chip, cc):
        first = cc * rows + (chip % 2) * (rows // 2) + (chip // 2) * per_dev
        return pl.ds(pl.multiple_of(first, per_dev), per_dev)

    def t_rows(chip, cc):
        return tall.at[t_first(chip, cc), :]

    def holder(chip):
        found = jnp.int32(0)
        for index in range(slots):
            found = jnp.where(slot_ref[index] == chip, index, found)
        return found

    pitch = prod.shape[0] // per_dev

    def project(chips):
        held = [holder(chip) for chip in chips]
        for e in range(per_dev):
            left = jnp.concatenate([act[e, h] for h in held], axis=0)
            right = jnp.concatenate([grad[e, h] for h in held], axis=0)
            left = jnp.where(positions < len_ref[e], left, jnp.zeros_like(left))
            prod[pl.ds(e * pitch, 4 * rank), :] = lax.dot_general(
                left, right, (((1,), (1,)), ((), ())), preferred_element_type=F32
            )
        for r in range(4):
            for g in range(proj // (4 * rank)):
                halves = []
                for h in range(per_dev // 8):
                    merged = None
                    for b in range(4):
                        row = h * 8 * pitch + r * rank + 4 * g + b
                        piece = prod[pl.ds(row, 8, stride=pitch), :]
                        if b != r:
                            piece = pltpu.roll(piece, ((b - r) % 4) * rank, 1)
                        merged = piece if merged is None else jnp.where(lanes == b, piece, merged)
                    halves.append(merged)
                tsend[chips[r], :, pl.ds(g * 4 * rank, 4 * rank)] = jnp.concatenate(
                    halves, axis=0
                ).astype(BF16)

    def t_to(chip):
        return remote(
            tsend.at[chip], t_rows(slot, core), t_send.at[chip], t_recv.at[slot],
            device(z, chip, core),
        )

    def q_part(plane):
        return qfull.at[pl.ds(pl.multiple_of((plane * 2 + core) * band, band), band), :]

    dp_rows = pl.ds(pl.multiple_of(dp * band, band), band)

    def q_first(count):
        mark = -count % planes
        return remote(qsrc, qfull.at[dp_rows, :], q_send.at[mark], q_recv.at[mark], twin(count))

    q_home = remote(q_part(z), q_part(z), q_send.at[0], q_recv.at[0], sibling)

    def sized(act_on, cc):
        pl.when(cc == 0)(lambda: act_on(kept))
        pl.when(cc == 1)(lambda: act_on(kept - 128))

    def gather(part, send, recv, share, run):
        def carried(offset, count, width):
            block = part(along(offset), width)
            mark = (offset - count) % planes
            return remote(block, block, send.at[mark], recv.at[mark], off(count))

        def arrived(mark, width):
            block = part(along(mark), width)
            return remote(block, block, send.at[mark], recv.at[mark], sibling)

        def last(width):
            block = part(along(FAR * way), width)
            return remote(block, block, send.at[8], recv.at[8], off(-3 * way))

        def across(mark, width):
            block = part(along(mark), width)
            return remote(
                block, block, send.at[planes + mark], recv.at[planes + mark], sibling
            )

        rest = [n % planes for n in (1, -1, 2, -2, 6, -6, 4, -4, 7, -7, 3, -3, 8)]

        def begin(width):
            for count in (FAR, -FAR) + NEAR:
                carried(0, count, width).start()

        def go_on(width):
            for offset in (FAR, -FAR):
                arrived(offset % planes, width).wait_recv()
                for count in NEAR:
                    carried(offset, count, width).start()
            last(width).start()
            if share:
                for mark in (0, FAR, planes - FAR):
                    across(mark, width).start()

        def finish(width):
            for mark in rest:
                arrived(mark, width).wait_recv()
                if share:
                    across(mark, width).start()
            if share:
                for mark in [0, FAR, planes - FAR] + rest:
                    across(mark, width).wait_send()
            for count in (FAR, -FAR) + NEAR:
                carried(0, count, width).wait_send()
            for offset in (FAR, -FAR):
                for count in NEAR:
                    carried(offset, count, width).wait_send()
            last(width).wait_send()

        def shared(width):
            for mark in [0, FAR, planes - FAR] + rest:
                block = share(along(mark), width)
                remote(
                    block, block, send.at[planes + mark], recv.at[planes + mark], sibling
                ).wait_recv()

        def finish_all():
            run(finish, core)
            if share:
                run(shared, 1 - core)

        return lambda: run(begin, core), lambda: run(go_on, core), finish_all

    def whole(act_on, cc):
        act_on(None)

    def q_other(plane, width):
        return qfull.at[pl.ds(pl.multiple_of((plane * 2 + 1 - core) * band, band), band), :]

    def g_part(cc):
        return lambda plane, width: gcirc.at[
            pl.ds(pl.multiple_of(cc * half + plane * band, band), band), pl.ds(0, width)
        ]

    _, q_go_on, q_finish = gather(
        lambda plane, width: q_part(plane), q_send, q_recv, q_other, whole
    )
    d_begin, d_go_on, d_finish = gather(
        lambda plane, width: plane_diags.at[plane], d_send, d_recv, None, whole
    )
    g_begin, g_go_on, g_finish = gather(g_part(core), g_send, g_recv, g_part(1 - core), sized)

    def chips_of(k, sign):
        chips = []
        for r in range(4):
            x, y = (slot // 4 + 4 + sign * r) % 4, (slot + 4 + sign * ((r + k) % 4)) % 4
            chips.append(x * 4 + y)
        return chips

    def scatter(chips):
        for r in (2, 1, 3, 0):

            @pl.when(chips[r] != slot)
            def _():
                t_to(chips[r]).start()

    def group(k, carry):
        project(chips_of(k, 1))
        return carry

    lax.fori_loop(1, slots // 4 + 1, group, 0)
    pl.semaphore_wait(barrier, 2 * slots - 1 + 14)

    def spread(k, carry):
        scatter(chips_of(k, 1))
        return carry

    lax.fori_loop(1, slots // 4 + 1, spread, 0)
    for count in (FAR, -FAR) + NEAR:
        q_first(count).start()

    @pl.when(y_lo != core)
    def _():
        q_first(0).start()

    @pl.when(y_lo == core)
    def _():
        qfull[dp_rows, :] = qsrc[...]

    tall[t_first(slot, core), :] = tsend[slot]

    def collect(k, carry):
        chips = chips_of(k, -1)
        for r in (1, 3, 2, 0):
            chip = chips[r]

            @pl.when(chip != slot)
            def _():
                remote(
                    t_rows(chip, core), t_rows(chip, core), t_send.at[chip], t_recv.at[chip],
                    sibling,
                ).wait_recv()

            remote(
                t_rows(chip, core), t_rows(chip, core), tsib_send.at[chip], tsib_recv.at[chip],
                sibling,
            ).start()
        return carry

    lax.fori_loop(1, 3, collect, 0)
    pl.when(y_lo != core)(lambda: q_home.wait_recv())
    q_go_on()
    lax.fori_loop(3, slots // 4 + 1, collect, 0)

    def collected(chip, carry):
        other = remote(
            t_rows(chip, 1 - core), t_rows(chip, 1 - core), tsib_send.at[chip], tsib_recv.at[chip],
            sibling,
        )
        other.wait_recv()
        other.wait_send()
        return carry

    lax.fori_loop(0, slots, collected, 0)

    apart = lax.broadcasted_iota(jnp.int32, (128, 128), 0) != lax.broadcasted_iota(
        jnp.int32, (128, 128), 1
    )
    per_block = 128 // band

    def columns(start, count):
        return tall[:, pl.ds(pl.multiple_of(start, 128), count)]

    def store(n, offset, value):
        for q in range(per_block):
            piece = value[q * band : (q + 1) * band]
            gpart[n * per_block + q, :, pl.ds(offset, value.shape[1])] = piece
            gsend[n * per_block + q, :, pl.ds(offset, value.shape[1])] = piece.astype(BF16)

    for n in range(half // 128):
        first = core * half + n * 128
        left = columns(first, 128)
        direct = half - n * 128
        value = lax.dot_general(
            left, columns(first, direct), (((0,), (0,)), ((), ())), preferred_element_type=F32
        )
        store(n, 0, jnp.where(apart, value[:, :128], 0.0))
        if direct > 128:
            store(n, 128, value[:, 128:])
        value = lax.dot_general(
            left, columns((1 - core) * half, kept - direct), (((0,), (0,)), ((), ())),
            preferred_element_type=F32,
        )
        store(n, direct, value)

    def near_send(count, a, width):
        index = NEAR.index(count) * 3 + a + 1
        cols = pl.ds(0, width)
        return remote(
            gsend.at[along(count - FAR * a), :, cols], near_in.at[index, :, cols],
            rs_send.at[index], rs_recv.at[index], off(count),
        )

    extra = 3 * len(NEAR)

    def last_send(width):
        cols = pl.ds(0, width)
        return remote(
            gsend.at[along(8), :, cols], near_in.at[extra, :, cols], rs_send.at[extra],
            rs_recv.at[extra], off(-3 * way),
        )

    def far_send(a, width):
        index = extra + 1 + (a + 1) // 2
        cols = pl.ds(0, width)
        return remote(
            far_out.at[(a + 1) // 2, :, cols], far_in.at[(a + 1) // 2, :, cols],
            rs_send.at[index], rs_recv.at[index], off(-FAR * a),
        )

    def near_start(width):
        for count in NEAR:
            for a in (1, -1):
                near_send(count, a, width).start()
        last_send(width).start()

    sized(near_start, core)

    @pl.when(core == 1)
    def _():
        near_in[:, :, pl.ds(kept - 128, 128)] = jnp.zeros((extra + 1, band, 128), BF16)
        far_in[:, :, pl.ds(kept - 128, 128)] = jnp.zeros((2, band, 128), BF16)

    squares = tall[...].astype(F32)
    squares = jnp.sum(squares * squares, axis=0, keepdims=True)
    for n in range(blocks):
        plane_diags[z, pl.ds(n, 1), :] = squares[:, n * 128 : (n + 1) * 128]
    d_begin()

    def window(a):
        value = gpart[along(-FAR * a)]
        for count in NEAR:
            value = value + near_in[NEAR.index(count) * 3 + a + 1].astype(F32)
        return value

    def near_wait(a):
        def wait(width):
            for count in NEAR:
                near_send(count, a, width).wait_recv()
            if a == -1:
                last_send(width).wait_recv()

        return wait

    sized(near_wait(1), core)
    upward = window(1)
    sized(near_wait(-1), core)
    downward = window(-1)
    more = near_in[extra].astype(F32)
    far_out[1] = (upward + jnp.where(core == 0, more, 0.0)).astype(BF16)
    far_out[0] = (downward + jnp.where(core == 0, 0.0, more)).astype(BF16)

    def far_start(width):
        for a in (1, -1):
            far_send(a, width).start()
        for count in NEAR:
            near_send(count, 0, width).start()

    sized(far_start, core)
    d_go_on()
    sized(near_wait(0), core)
    value = window(0)


    def far_wait(width):
        for a in (1, -1):
            far_send(a, width).wait_recv()

    sized(far_wait, core)
    value = value + far_in[1].astype(F32) + far_in[0].astype(F32)
    gcirc[pl.ds(pl.multiple_of(core * half + z * band, band), band), :] = value.astype(BF16)
    g_begin()

    d_finish()
    diagonal = jnp.sum(plane_diags[...], axis=0) / examples
    own_eig = jnp.sum(jnp.sum(diagonal, axis=1, keepdims=True), axis=0, keepdims=True) / proj
    slot_traces[slot] = jnp.broadcast_to(own_eig, (8, 128))
    diag_ref[...] = jnp.concatenate([diagonal[n : n + 1] for n in range(blocks)], axis=1)

    def trace_to(chip):
        return remote(
            slot_traces.at[slot], slot_traces.at[slot], tr_send.at[chip], tr_recv.at[slot],
            device(z, chip, core),
        )

    def trace_from(chip):
        return remote(
            slot_traces.at[chip], slot_traces.at[chip], tr_send.at[chip], tr_recv.at[chip], sibling
        )

    def tell(k, carry):
        trace_to((slot + k) % slots).start()
        return carry

    lax.fori_loop(1, slots, tell, 0)
    g_go_on()

    def settle(k, carry):
        chip = (slot + k) % slots
        t_to(chip).wait_send()
        trace_to(chip).wait_send()
        trace_from(chip).wait_recv()
        return carry

    lax.fori_loop(1, slots, settle, 0)
    pl.when(y_lo != core)(lambda: q_first(0).wait_send())

    def sums_sent(width):
        for count in NEAR:
            for a in (1, -1, 0):
                near_send(count, a, width).wait_send()
        last_send(width).wait_send()
        for a in (1, -1):
            far_send(a, width).wait_send()

    sized(sums_sent, core)
    q_finish()
    g_finish()

    for n in range(blocks):
        for k in range(kept // 128):
            other = (n + k) % blocks
            if 2 * k == blocks and n >= other:
                continue
            piece = gcirc[n * 128 : (n + 1) * 128, k * 128 : (k + 1) * 128]
            gfull[n * 128 : (n + 1) * 128, other * 128 : (other + 1) * 128] = piece
            if k > 0:
                gfull[other * 128 : (other + 1) * 128, n * 128 : (n + 1) * 128] = piece.T

    damping = 0.1 * (jnp.sum(slot_traces[...], axis=0)[0:1, 0:1] / slots)
    upper = damping + 4.0 * own_eig
    center = (upper + damping) / 2.0
    radius = (upper - damping) / 2.0
    sigma = center / radius
    rho = 1.0 / sigma
    train = tall[pl.ds(pl.multiple_of(core * rows, rows), rows), :].astype(F32)
    resid_ref[...] = train
    step_ref[...] = train / center
    acc_ref[...] = step_ref[...]
    tile = min(256, proj)
    for index in range(ITERS - 1):
        rho_next = 1.0 / (2.0 * sigma - rho)
        rounded = step_ref[...].astype(BF16)

        for n in range(proj // tile):
            cols = pl.ds(n * tile, tile)
            product = jnp.dot(rounded, gfull[:, cols], preferred_element_type=F32)
            step = step_ref[:, cols]
            resid = resid_ref[:, cols] - (
                product * (1.0 / examples) + (diag_ref[:, cols] + damping) * step
            )
            resid_ref[:, cols] = resid
            step = rho_next * rho * step + (2.0 * rho_next / radius) * resid
            step_ref[:, cols] = step
            acc_ref[:, cols] = acc_ref[:, cols] + step
        rho = rho_next

    scores = jnp.dot(acc_ref[...].astype(BF16), qfull[...], preferred_element_type=F32)
    ssend[...] = scores.T.astype(BF16)

    def block(index):
        owner, low = index // 2, index % 2
        return ssend.at[
            pl.ds(pl.multiple_of(owner * per_owner, per_owner), per_owner),
            pl.ds(pl.multiple_of(low * (rows // 2), rows // 2), rows // 2),
        ]

    mark = slot * 2 + core

    def score_to(index):
        return remote(
            block(index), srecv.at[mark], s_send.at[index], s_recv.at[mark],
            (z * 2 + index % 2, index // 2),
        )

    own = mod * 2 + y_lo

    def push(k, carry):
        index = (own + k) % (2 * slots)
        score_to(index).start()
        return carry

    lax.fori_loop(1, 2 * slots, push, 0)
    srecv[mark] = ssend[
        pl.ds(pl.multiple_of(mod * per_owner, per_owner), per_owner),
        pl.ds(pl.multiple_of(y_lo * (rows // 2), rows // 2), rows // 2),
    ]

    def pull(k, carry):
        index = (mark + k) % (2 * slots)
        remote(
            srecv.at[index], srecv.at[index], s_send.at[index], s_recv.at[index], sibling
        ).wait_recv()
        return carry

    lax.fori_loop(1, 2 * slots, pull, 0)
    sums = []
    for cc in range(2):
        summed = srecv[cc].astype(F32)
        for chip in range(1, slots):
            summed = summed + srecv[chip * 2 + cc].astype(F32)
        sums.append(summed)
    width = rows // 2
    runs = width // per_dev
    lane_run = lax.broadcasted_iota(jnp.int32, (per_owner, width), 1) // per_dev
    for h in range(2):
        merged = jnp.zeros((per_owner, width), F32)
        for n in range(runs // 2):
            for cc in range(2):
                shift = (2 * n + cc - (h * (runs // 2) + n)) % runs
                piece = pltpu.roll(sums[cc], shift * per_dev, 1) if shift else sums[cc]
                merged = jnp.where(lane_run == 2 * n + cc, piece, merged)
        out_ref[:, pl.ds(h * width, width)] = merged

    def pushed(k, carry):
        score_to((own + k) % (2 * slots)).wait_send()
        return carry

    lax.fori_loop(1, 2 * slots, pushed, 0)


def per_device(planes, act_factors, grad_factors, lengths, module_slot, query_grads):
    per_dev, slots, rank, span = act_factors.shape
    proj = rank * rank
    rows = slots * per_dev
    band, queries = query_grads.shape[1:]
    per_owner = queries // slots
    kept = (proj // 128 // 2 + 1) * 128
    sem = pltpu.SemaphoreType.DMA
    vmem = pltpu.VMEM
    result = pl.pallas_call(
        functools.partial(kernel, planes),
        out_shape=jax.ShapeDtypeStruct((per_owner, rows), F32),
        in_specs=[
            pl.BlockSpec(memory_space=pltpu.SMEM),
            pl.BlockSpec(memory_space=pltpu.SMEM),
            pl.BlockSpec(memory_space=pltpu.HBM),
            pl.BlockSpec(memory_space=pltpu.HBM),
            pl.BlockSpec(memory_space=pltpu.VMEM),
        ],
        out_specs=pl.BlockSpec(memory_space=pltpu.VMEM),
        scratch_shapes=[
            vmem((per_dev, slots, rank, span), BF16),
            vmem((per_dev, slots, rank, span), BF16),
            vmem((per_dev * (4 * rank + 8), 4 * rank), F32),
            vmem((slots, per_dev, proj), BF16),
            vmem((2 * rows, proj), BF16),
            vmem((planes, band, kept), F32),
            vmem((proj, kept), BF16),
            vmem((proj, proj), BF16),
            vmem((planes, band, kept), BF16),
            vmem((13, band, kept), BF16),
            vmem((2, band, kept), BF16),
            vmem((2, band, kept), BF16),
            vmem((band, queries), BF16),
            vmem((proj, queries), BF16),
            vmem((rows, proj), F32),
            vmem((rows, proj), F32),
            vmem((rows, proj), F32),
            vmem((queries, rows), BF16),
            vmem((2 * slots, per_owner, rows // 2), BF16),
            vmem((slots, 8, 128), F32),
            vmem((planes, proj // 128, 128), F32),
            vmem((1, proj), F32),
            sem((LOADS, 2)),
            sem((slots,)),
            sem((slots,)),
            sem((slots,)),
            sem((slots,)),
            sem((2 * planes,)),
            sem((2 * planes,)),
            sem((15,)),
            sem((15,)),
            sem((2 * planes,)),
            sem((2 * planes,)),
            sem((planes,)),
            sem((planes,)),
            sem((slots,)),
            sem((slots,)),
            sem((2 * slots,)),
            sem((2 * slots,)),
        ],
        compiler_params=pltpu.CompilerParams(
            collective_id=0, has_side_effects=True, vmem_limit_bytes=62 * 1024 * 1024
        ),
    )(module_slot, lengths, act_factors, grad_factors, query_grads[0])
    return result.T


def solution(mesh):
    planes = mesh.shape["dp"] // 2
    return jax.shard_map(
        functools.partial(per_device, planes),
        mesh=mesh,
        in_specs=(
            P(("dp", "module"), None, None, None),
            P(("dp", "module"), None, None, None),
            P(("dp", "module")),
            P(),
            P("module", "dp", None),
        ),
        out_specs=P("dp", "module"),
        check_vma=False,
    )
```
